32 devices in a mesh: groups: 2 (over y), trade: 4 (over z), date: 2 (over x), scen: 2 (over core).
Axes of the slice: x: 2, y: 2, z: 4, core: 2. Of those that a mesh axis runs over, the one named last changes fastest.
Arguments:
- cash_flows: bfloat16 [1024, 64], P('trade'), may hold values from -0.8984375 to 0.8984375
- coupon_dates: int32 [1024, 64], P('trade'), may hold values from 0 to 127, as said below
- trade_sets: int32 [1024], P('trade'), may hold values from 0 to 511, as said below
- set_slots: int32 [512], replicated, may hold values from 0 to 511, as said below
- set_lags: int32 [512], P('trade'), may hold values from 0 to 4
- thresholds: float32 [512], P('trade'), may hold values from 0.05 to 1
- set_cpty: int32 [512], P('trade'), may hold values from 0 to 127
- discounts: bfloat16 [128, 128, 512], P('date', None, ('groups', 'scen')), parts along dimension 2, may hold values from 0.29882812 to 1
- default_probs: float32 [128, 128], P(None, 'date'), may hold values from 0.004 to 0.04
- loss_given: float32 [128], replicated, may hold values from 0.4 to 0.9
- cva_cotangent: float32 [128], replicated, may hold values from -6 to 6
Outputs:
- credit_charge: float32 [256], P('groups'), parts along dimension 0
- flow_grads: float32 [2048, 64], P(('groups', 'trade')), parts along dimension 0
The draws below stay inside these ranges and needn't reach their ends.
There are 2 independent parts, one for each index of `groups`. The reference program is written for one: setup_inputs(seed, part) draws one part's arguments, and reference() takes and returns one part's arrays. A program takes and returns all parts, laid end to end along the dimension named above; an argument that names none is the same for every part. Nothing has to cross between parts.
Inputs may be any that keep to these rules, and one draw needn't show every extreme that they name: `coupon_dates`: the 64 dates of one swap are distinct. Call set_slots[trade_sets[n]] // 128 the owner of swap n; among the 256 swaps of one device at most 128 have the same owner, and some owner has exactly 128 swaps of every device. `set_slots`: each position is taken by exactly one netting set.
All inputs are finite; a program needn't handle non-finite values.
Results may differ from the reference program's by a relative error of at most 0.0027.
Values may be sent and summed in bfloat16 or wider, within the bound.
A program may use at most 128 MiB of HBM per device.

```python
import math
import jax
import jax.numpy as jnp
from jax import lax

DATES = 128
COUPONS = 64
LAGMAX = 4
TR_DEV = 256
NS_DEV = 128
TRADES = 1024
NSETS = 512
CPTY = 128
SCEN = 256
CAP = 128


def trade_layout(key):
    owner_count = TRADES // TR_DEV
    buckets = owner_count * CAP
    key_list = jax.random.split(key, 5)
    set_order = jax.random.permutation(key_list[0], NSETS).astype(jnp.int32)
    crowded = jax.random.randint(key_list[1], (), 0, owner_count)
    places = jnp.arange(buckets, dtype=jnp.int32)
    scores = jax.random.randint(key_list[2], (owner_count, buckets), 0, 2 ** 16) * buckets + places[None, :]
    scores = jnp.where((places // CAP == crowded)[None, :], places[None, :] - buckets, scores)
    chosen = jnp.argsort(scores, axis=1)[:, :TR_DEV].astype(jnp.int32)
    mixing = jax.random.randint(key_list[3], (owner_count, TR_DEV), 0, 2 ** 16) * TR_DEV + jnp.arange(TR_DEV, dtype=jnp.int32)[None, :]
    chosen = jnp.take_along_axis(chosen, jnp.argsort(mixing, axis=1), axis=1)
    row_picks = jax.random.randint(key_list[4], (owner_count, TR_DEV), 0, NS_DEV)
    stored = chosen // CAP * NS_DEV + row_picks
    named_ids = jnp.zeros((NSETS,), jnp.int32).at[set_order].set(jnp.arange(NSETS, dtype=jnp.int32))
    return (named_ids[stored.reshape(-1)].astype(jnp.int32), set_order)


def draw_trade_sets(key, part):
    shared = trade_layout(key)
    return shared[0]


def draw_set_slots(key, part):
    shared = trade_layout(key)
    return shared[1]


def draw_coupon_dates(key, part):
    key = jax.random.fold_in(key, 7)
    scores = jax.random.randint(key, (TRADES, DATES), 0, 2 ** 20) * DATES + jnp.arange(DATES, dtype=jnp.int32)[None, :]
    ordering = jnp.argsort(scores, axis=1)[:, :COUPONS]
    return jnp.sort(ordering, axis=1).astype(jnp.int32)


def set_ends(array, key, smallest, largest):
    longest = array.shape.index(max(array.shape))
    spots = []
    for shift in (0, 1):
        where = [jax.random.randint(jax.random.fold_in(key, axis), (), 0, length) for axis, length in enumerate(array.shape)]
        where[longest] = (where[longest] + shift) % array.shape[longest]
        spots.append(tuple(where))
    return array.at[spots[0]].set(smallest).at[spots[1]].set(largest)


def block_scale(key, extent, cuts, low, largest):
    loudness, own = 1.0, jax.random.fold_in(key, 6)
    for dim, shards_of in cuts:
        heights = jnp.exp(jax.random.uniform(jax.random.fold_in(own, dim), (shards_of,), jnp.float32, low / len(cuts), largest / len(cuts)))
        loudness = loudness * jnp.repeat(heights, extent[dim] // shards_of).reshape([-1 if axis == dim else 1 for axis in range(len(extent))])
    return loudness


def scatter_about(rng, extent, width, bound, cuts=(), kind=jnp.bfloat16):
    drawn = jax.random.normal(rng, extent, jnp.float32) * width
    if len(cuts) > 0:
        drawn = block_scale(rng, extent, cuts, -0.22, 0.18) * drawn
    return jnp.clip(drawn, min=-bound, max=bound).astype(kind)


def setup_inputs(seed: int = 0, part: int = 0) -> dict:
    arg_keys = jax.random.split(jax.random.key(seed), 12)
    part_keys = jax.random.split(jax.random.fold_in(arg_keys[11], part), 12)
    return {
        "cash_flows": scatter_about(arg_keys[0], (TRADES, COUPONS), 0.15, 0.8984375, ((0, 4),)),
        "coupon_dates": draw_coupon_dates(jax.random.fold_in(arg_keys[11], 71), part),
        "trade_sets": draw_trade_sets(jax.random.fold_in(arg_keys[11], 71), part),
        "set_slots": draw_set_slots(jax.random.fold_in(arg_keys[11], 71), part),
        "set_lags": set_ends(jax.random.randint(arg_keys[4], (NSETS,), 0, LAGMAX + 1), jax.random.fold_in(arg_keys[4], 1), 0, LAGMAX).astype(jnp.int32),
        "thresholds": jnp.clip(0.05 + 0.95 * jax.random.uniform(arg_keys[5], (NSETS,), jnp.float32) ** block_scale(arg_keys[5], (NSETS,), ((0, 4),), -0.2, 0.2), 0.05, 1.0),
        "set_cpty": set_ends(jax.random.randint(arg_keys[6], (NSETS,), 0, CPTY), jax.random.fold_in(arg_keys[6], 1), 0, CPTY - 1).astype(jnp.int32),
        "discounts": jnp.clip(0.29882812 + 0.7011719 * jax.random.uniform(part_keys[7], (DATES, DATES, SCEN), jnp.float32) ** block_scale(part_keys[7], (DATES, DATES, SCEN), ((0, 2), (2, 2)), -0.2, 0.2), 0.29882812, 1.0).astype(jnp.bfloat16),
        "default_probs": jnp.clip(jnp.exp(math.log(0.04) - 2.30258502 * jax.random.uniform(arg_keys[8], (CPTY, DATES), jnp.float32) ** block_scale(arg_keys[8], (CPTY, DATES), ((1, 2),), -0.2, 0.2)), 0.004, 0.04),
        "loss_given": jnp.clip(jax.random.uniform(arg_keys[9], (CPTY,), jnp.float32, 0.4, 0.9), 0.4, 0.9),
        "cva_cotangent": scatter_about(arg_keys[10], (CPTY,), 1.0, 6.0, (), jnp.float32),
    }


SMOOTH = 0.1


def coupon_grid(cash_flows, coupon_dates):
    date_axis = jnp.arange(DATES, dtype=jnp.int32)

    def per_block(inputs):
        amounts, moments = inputs
        matched = moments[:, :, None] == date_axis[None, None, :]
        return jnp.sum(jnp.where(matched, amounts.astype(jnp.float32)[:, :, None], jnp.float32(0.0)), axis=1)

    blocks = (cash_flows.reshape(-1, TR_DEV, COUPONS), coupon_dates.reshape(-1, TR_DEV, COUPONS))
    return lax.map(per_block, blocks).reshape(TRADES, DATES)


def reference(cash_flows, coupon_dates, trade_sets, set_slots, set_lags, thresholds, set_cpty, discounts, default_probs, loss_given, cva_cotangent):
    positions = set_slots[trade_sets].astype(jnp.int32)
    trade_flows = coupon_grid(cash_flows, coupon_dates).astype(jnp.bfloat16)
    set_flows = jax.ops.segment_sum(trade_flows.astype(jnp.float32), positions, num_segments=NSETS).astype(jnp.bfloat16)
    date_axis = jnp.arange(DATES, dtype=jnp.int32)
    is_later = date_axis[None, :, None] > date_axis[:, None, None]
    forward = jnp.where(is_later, discounts, jnp.zeros((), jnp.bfloat16)).astype(jnp.float32)

    def per_sets(inputs):
        block_flows, block_lags, block_limits, block_owners = inputs
        values = jnp.einsum("pu,tus->pts", block_flows.astype(jnp.float32), forward)
        padded = jnp.concatenate([jnp.zeros((NS_DEV, LAGMAX, SCEN), jnp.float32), values], axis=1)
        where_from = (LAGMAX + date_axis[None, :] - block_lags[:, None]).astype(jnp.int32)
        lagged = jnp.take_along_axis(padded, jnp.broadcast_to(where_from[:, :, None], values.shape), axis=1)
        in_range = (date_axis[None, :] >= block_lags[:, None])[:, :, None]
        over_limit = (lagged - block_limits[:, None, None]) / SMOOTH
        collateral = jnp.where(in_range, SMOOTH * jax.nn.softplus(over_limit), jnp.float32(0.0))
        margin_gap = values - collateral
        exposure = SMOOTH * jax.nn.softplus(margin_gap / SMOOTH)
        exposure_curve = jnp.mean(exposure, axis=2)
        hazard_intensity = default_probs[block_owners]
        losses = loss_given[block_owners]
        netting_set_contributions = losses * jnp.sum(hazard_intensity * exposure_curve, axis=1)
        partial_charge = jax.ops.segment_sum(netting_set_contributions, block_owners, num_segments=CPTY)
        netting_set_gather = (cva_cotangent[block_owners] * losses)[:, None] * hazard_intensity / SCEN
        direct = netting_set_gather[:, :, None] * jax.nn.sigmoid(margin_gap / SMOOTH)
        backward = jnp.where(in_range, -direct * jax.nn.sigmoid(over_limit), jnp.float32(0.0))
        carried = jnp.zeros((NS_DEV, LAGMAX + DATES, SCEN), jnp.float32)
        for offset in range(LAGMAX + 1):
            picked = jnp.where((block_lags == offset)[:, None, None], backward, jnp.float32(0.0))
            carried = carried + jnp.pad(picked, ((0, 0), (LAGMAX - offset, offset), (0, 0)))
        value_grads = (direct + carried[:, LAGMAX:]).astype(jnp.bfloat16)
        set_grads = jnp.einsum("pts,tus->pu", value_grads.astype(jnp.float32), forward)
        return partial_charge, set_grads

    blocks = (set_flows.reshape(-1, NS_DEV, DATES), set_lags.reshape(-1, NS_DEV), thresholds.reshape(-1, NS_DEV), set_cpty.reshape(-1, NS_DEV))
    charges, grad_blocks = lax.map(per_sets, blocks)
    credit_charge = jnp.sum(charges, axis=0)
    set_grads = grad_blocks.reshape(NSETS, DATES)
    trade_grads = set_grads[positions]
    flow_grads = jnp.take_along_axis(trade_grads, coupon_dates, axis=1)
    return credit_charge, flow_grads
```

```python
import functools

import jax
import jax.numpy as jnp
from jax import lax
from jax.experimental import pallas as pl
from jax.experimental.pallas import tpu as pltpu
from jax.sharding import PartitionSpec as P

LAGMAX = 4
RATE = 10.0
STEP = 4
MESH = pl.DeviceIdType.MESH
NT = (((1,), (1,)), ((), ()))
F32 = jnp.float32
BF16 = jnp.bfloat16


def smooth(a):
    s = 0.5 + 0.5 * jnp.tanh(0.5 * jnp.abs(a))
    return jnp.maximum(a, 0.0) - jnp.log(s), jnp.where(a >= 0.0, s, 1.0 - s)


def exact_dot(a, b, dims=(((1,), (0,)), ((), ()))):
    return lax.dot_general(a, b, dims, precision=lax.Precision.HIGHEST, preferred_element_type=F32)


def kernel(
    n_trade,
    n_date,
    n_scen,
    cash_ref,
    dates_ref,
    sets_ref,
    slots_ref,
    lags_ref,
    limits_ref,
    cpty_ref,
    probs_ref,
    loss_ref,
    cot_ref,
    market_ref,
    charge_ref,
    flows_ref,
    fwd,
    fwd_t,
    vals,
    coll,
    gate,
    direct,
    hazard,
    weight,
    member,
    parts_out,
    parts_in,
    set_flows,
    total,
    total_in,
    every,
    trade_rows,
    charge_out,
    charge_in,
    charge_sum,
    charge_far,
    load_sem,
    halo_sem,
    parts_sem,
    flow_sem,
    total_sem,
    charge_sem,
    far_sem,
    every_z_sem,
    every_g_sem,
):
    z = lax.axis_index("trade")
    d = lax.axis_index("date")
    c = lax.axis_index("scen")
    n_group = n_date * n_scen
    g = d * n_scen + c
    span, n_u, n_s = market_ref.shape
    n_p = lags_ref.shape[1]
    n_sets = slots_ref.shape[1]
    n_c = probs_ref.shape[1]
    n_n = sets_ref.shape[1]
    n_k = dates_ref.shape[0]
    uq = n_u // n_group
    steps = span + LAGMAX
    first = d * span

    def trade_peer(k):
        return {"trade": lax.rem(z + k, n_trade)}

    def group_peer(k):
        peer = lax.rem(g + k, n_group)
        return {"date": peer // n_scen, "scen": lax.rem(peer, n_scen)}

    def send(src, dst, sems, index, device):
        copy = pltpu.make_async_remote_copy(
            src_ref=src,
            dst_ref=dst,
            send_sem=sems.at[(0,) + index],
            recv_sem=sems.at[(1,) + index],
            device_id=device,
            device_id_type=MESH,
        )
        copy.start()
        return copy

    barrier = pltpu.get_barrier_semaphore()
    for k in range(1, n_trade):
        pl.semaphore_signal(barrier, inc=1, device_id=trade_peer(k), device_id_type=MESH)
    for k in range(1, n_group):
        pl.semaphore_signal(barrier, inc=1, device_id=group_peer(k), device_id_type=MESH)

    load = pltpu.make_async_copy(market_ref, fwd.at[pl.ds(LAGMAX, span)], load_sem)
    load.start()

    mine = pl.multiple_of(g * uq, uq)
    u_rows = lax.broadcasted_iota(jnp.int32, (uq, n_n), 0) + g * uq
    grid = jnp.zeros((uq, n_n), F32)
    cash = cash_ref[...].astype(F32)
    moments = dates_ref[...]
    for k in range(n_k):
        grid = jnp.where(u_rows == moments[k : k + 1, :], cash[k : k + 1, :], grid)

    wanted = lax.broadcasted_iota(jnp.int32, (n_sets, n_n), 0) == sets_ref[...]
    slots = slots_ref[...]
    digit = lax.broadcasted_iota(jnp.int32, (8, n_sets), 0)
    digits = jnp.where(digit == 0, slots >> 6, jnp.where(digit == 1, slots & 63, 0))
    found = jnp.dot(digits.astype(F32).astype(BF16), wanted.astype(F32).astype(BF16), preferred_element_type=F32)
    positions = (found[0:1, :] * 64.0 + found[1:2, :]).astype(jnp.int32)
    p_rows = lax.broadcasted_iota(jnp.int32, (n_sets, n_n), 0)
    member[...] = (p_rows == positions).astype(F32).astype(BF16)
    partial = lax.dot_general(grid.astype(BF16), member[...], NT, preferred_element_type=F32)
    for o in range(n_trade):
        parts_out[o] = partial[:, o * n_p : (o + 1) * n_p]

    pl.semaphore_wait(barrier, n_trade - 1 + n_group - 1)
    pending = []
    arrivals = []
    for k in range(1, n_trade):
        to = lax.rem(z + k, n_trade)
        arrivals.append(send(parts_out.at[to], parts_in.at[k], parts_sem, (k,), trade_peer(k)))
    next_date = {"date": lax.rem(d + 1, n_date)}
    halo = send(
        market_ref.at[pl.ds(span - LAGMAX, LAGMAX)], fwd.at[pl.ds(0, LAGMAX)], halo_sem, (), next_date
    )

    named = lax.broadcasted_iota(jnp.int32, (n_c, n_p), 0) == cpty_ref[...]
    named = named.astype(F32)
    loss = loss_ref[...]
    scale_row = lax.broadcasted_iota(jnp.int32, (8, n_c), 0)
    scales = jnp.where(scale_row == 0, loss, jnp.where(scale_row == 1, loss * cot_ref[...], 0.0))
    scales = exact_dot(scales, named)
    paths = float(n_s * n_scen)
    hazard[...] = exact_dot(probs_ref[...], named)
    weight[...] = hazard[...] * (scales[1:2, :] / paths)

    u_col = lax.broadcasted_iota(jnp.int32, (n_u, n_s), 0)

    def mask_dates(t, shown):
        later = (u_col > first + (t - LAGMAX)).astype(F32) * shown
        block = fwd[t] * later.astype(BF16)
        fwd[t] = block
        fwd_t[t] = block.T

    load.wait()

    def mask_step(i, carry):
        for b in range(STEP):
            mask_dates(LAGMAX + i * STEP + b, 1.0)
        return carry

    lax.fori_loop(0, span // STEP, mask_step, 0)

    for copy in arrivals:
        copy.wait_recv()
    pending += arrivals
    mine_sum = parts_out[z]
    for k in range(1, n_trade):
        mine_sum = mine_sum + parts_in[k]
    set_flows[pl.ds(mine, uq), :] = mine_sum.astype(BF16)
    arrivals = []
    for k in range(1, n_group):
        block = set_flows.at[pl.ds(mine, uq)]
        arrivals.append(send(block, block, flow_sem, (k,), group_peer(k)))

    halo.wait()
    after_first = jnp.where(d > 0, 1.0, 0.0).astype(F32)
    for b in range(LAGMAX):
        mask_dates(b, after_first)
    for copy in arrivals:
        copy.wait_recv()
    pending += arrivals

    flows = set_flows[...]
    limits = limits_ref[...] * RATE

    def value_date(t, shown):
        v = jnp.dot(fwd_t[t], flows, preferred_element_type=F32) * RATE
        amount, slope = smooth(v - limits)
        if shown is not None:
            amount, slope = amount * shown, slope * shown
        vals[t] = v
        coll[t] = amount
        gate[t] = slope

    for b in range(LAGMAX):
        value_date(b, after_first)

    def value_step(i, carry):
        for b in range(STEP):
            value_date(LAGMAX + i * STEP + b, None)
        return carry

    lax.fori_loop(0, span // STEP, value_step, 0)

    lags = lags_ref[...]

    def by_lag(rows):
        out = rows[0]
        for lag in range(1, LAGMAX + 1):
            out = jnp.where(lags == lag, rows[lag], out)
        return out

    for b in range(LAGMAX):
        direct[b] = jnp.zeros((n_s, n_p), F32)
        direct[steps + b] = jnp.zeros((n_s, n_p), F32)

    def exposure_step(i, acc):
        for b in range(STEP):
            own = i * STEP + b
            t = LAGMAX + own
            margin = vals[t] - by_lag([coll[t - lag] for lag in range(LAGMAX + 1)])
            amount, slope = smooth(margin)
            acc = acc + amount * hazard[pl.ds(own, 1), :]
            direct[t] = slope * weight[pl.ds(own, 1), :]
        return acc

    acc = lax.fori_loop(0, span // STEP, exposure_step, jnp.zeros((n_s, n_p), F32))
    terms = jnp.sum(acc, axis=0, keepdims=True) * (scales[0:1, :] * (1.0 / (RATE * paths)))
    charge_out[...] = exact_dot(jnp.broadcast_to(terms, (8, n_p)), named, NT)
    charges = []
    for k in range(1, n_group):
        charges.append(send(charge_out, charge_in.at[k], charge_sem, (k,), group_peer(k)))

    def grad_step(i, acc):
        for b in range(STEP):
            t = i * STEP + b
            later = by_lag([direct[t + lag] for lag in range(LAGMAX + 1)])
            block = (direct[t] - later * gate[t]).astype(BF16)
            acc = acc + jnp.dot(fwd[t], block, preferred_element_type=F32)
        return acc

    total[...] = lax.fori_loop(0, steps // STEP, grad_step, jnp.zeros((n_u, n_p), F32))

    arrivals = []
    for k in range(1, n_group):
        theirs = pl.multiple_of(lax.rem(g + k, n_group) * uq, uq)
        arrivals.append(
            send(total.at[pl.ds(theirs, uq)], total_in.at[k], total_sem, (k,), group_peer(k))
        )

    for copy in charges:
        copy.wait_recv()
    pending += charges
    group_charge = charge_out[...]
    for k in range(1, n_group):
        group_charge = group_charge + charge_in[k]
    charge_sum[...] = group_charge
    charges = []
    for k in range(1, n_trade):
        charges.append(send(charge_sum, charge_far.at[k], far_sem, (k,), trade_peer(k)))

    for copy in arrivals:
        copy.wait_recv()
    pending += arrivals
    mine_sum = total[pl.ds(mine, uq), :]
    for k in range(1, n_group):
        mine_sum = mine_sum + total_in[k]
    every[z, pl.ds(mine, uq), :] = mine_sum.astype(BF16)

    across = []
    block = every.at[z, pl.ds(mine, uq)]
    for k in range(1, n_trade):
        across.append(send(block, block, every_z_sem, (k,), trade_peer(k)))
    within = []
    for k in range(1, n_group):
        within.append(send(block, block, every_g_sem, (0, k), group_peer(k)))
    for j in range(1, n_trade):
        across[j - 1].wait_recv()
        block = every.at[lax.rem(z + n_trade - j, n_trade), pl.ds(mine, uq)]
        for k in range(1, n_group):
            within.append(send(block, block, every_g_sem, (j, k), group_peer(k)))
    pending += across

    for copy in charges:
        copy.wait_recv()
    pending += charges
    group_charge = charge_sum[...]
    for k in range(1, n_trade):
        group_charge = group_charge + charge_far[k]
    charge_ref[...] = group_charge[0:1, :]

    for copy in within:
        copy.wait_recv()
    pending += within
    rows = jnp.zeros((n_u, n_n), F32)
    for o in range(n_trade):
        rows = rows + jnp.dot(every[o], member[o * n_p : (o + 1) * n_p, :], preferred_element_type=F32)
    trade_rows[...] = rows

    def pick_step(i, out):
        base = pl.multiple_of(i * 8, 8)
        rows = trade_rows[pl.ds(base, 8), :]
        for b in range(8):
            out = jnp.where(moments == base + b, rows[b : b + 1, :], out)
        return out

    flows_ref[...] = lax.fori_loop(0, n_u // 8, pick_step, jnp.zeros((n_k, n_n), F32))
    for copy in pending:
        copy.wait_send()


def per_device(
    cash_flows,
    coupon_dates,
    trade_sets,
    set_slots,
    set_lags,
    thresholds,
    set_cpty,
    discounts,
    default_probs,
    loss_given,
    cva_cotangent,
):
    n_trade, n_date, n_scen = (lax.axis_size(a) for a in ("trade", "date", "scen"))
    n_group = n_date * n_scen
    n_n, n_k = cash_flows.shape
    span, n_u, n_s = discounts.shape
    n_p = set_lags.shape[0]
    n_sets = set_slots.shape[0]
    n_c = loss_given.shape[0]
    uq = n_u // n_group
    steps = span + LAGMAX
    vmem = pl.BlockSpec(memory_space=pltpu.VMEM)
    dma = pltpu.SemaphoreType.DMA
    charge, flow_grads = pl.pallas_call(
        functools.partial(kernel, n_trade, n_date, n_scen),
        out_shape=(
            jax.ShapeDtypeStruct((1, n_c), F32),
            jax.ShapeDtypeStruct((n_k, n_n), F32),
        ),
        in_specs=[vmem] * 10 + [pl.BlockSpec(memory_space=pl.ANY)],
        out_specs=(vmem, vmem),
        scratch_shapes=[
            pltpu.VMEM((steps, n_u, n_s), BF16),
            pltpu.VMEM((steps, n_s, n_u), BF16),
            pltpu.VMEM((steps, n_s, n_p), F32),
            pltpu.VMEM((steps, n_s, n_p), F32),
            pltpu.VMEM((steps, n_s, n_p), F32),
            pltpu.VMEM((steps + LAGMAX, n_s, n_p), F32),
            pltpu.VMEM((span, n_p), F32),
            pltpu.VMEM((span, n_p), F32),
            pltpu.VMEM((n_sets, n_n), BF16),
            pltpu.VMEM((n_trade, uq, n_p), F32),
            pltpu.VMEM((n_trade, uq, n_p), F32),
            pltpu.VMEM((n_u, n_p), BF16),
            pltpu.VMEM((n_u, n_p), F32),
            pltpu.VMEM((n_group, uq, n_p), F32),
            pltpu.VMEM((n_trade, n_u, n_p), BF16),
            pltpu.VMEM((n_u, n_n), F32),
            pltpu.VMEM((8, n_c), F32),
            pltpu.VMEM((n_group, 8, n_c), F32),
            pltpu.VMEM((8, n_c), F32),
            pltpu.VMEM((n_trade, 8, n_c), F32),
            dma,
            dma((2,)),
            dma((2, n_trade)),
            dma((2, n_group)),
            dma((2, n_group)),
            dma((2, n_group)),
            dma((2, n_trade)),
            dma((2, n_trade)),
            dma((2, n_trade, n_group)),
        ],
        compiler_params=pltpu.CompilerParams(
            collective_id=0, has_side_effects=True, vmem_limit_bytes=48 * 1024 * 1024
        ),
    )(
        cash_flows.T,
        coupon_dates.T,
        trade_sets.reshape(1, -1),
        set_slots.reshape(1, -1),
        set_lags.reshape(1, -1),
        thresholds.reshape(1, -1),
        set_cpty.reshape(1, -1),
        default_probs.T,
        loss_given.reshape(1, -1),
        cva_cotangent.reshape(1, -1),
        discounts,
    )
    return charge.reshape(-1), flow_grads.T


def solution(mesh):
    in_specs = (
        P("trade", None),
        P("trade", None),
        P("trade"),
        P(),
        P("trade"),
        P("trade"),
        P("trade"),
        P("date", None, ("groups", "scen")),
        P(None, "date"),
        P(),
        P(),
    )
    out_specs = (P("groups"), P(("groups", "trade"), None))
    return jax.shard_map(
        per_device, mesh=mesh, in_specs=in_specs, out_specs=out_specs, check_vma=False
    )
```

```python
import functools

import jax
import jax.numpy as jnp
from jax import lax
from jax.experimental import pallas as pl
from jax.experimental.pallas import tpu as pltpu
from jax.sharding import PartitionSpec as P

LAGMAX = 4
RATE = 10.0
STEP = 4
MESH = pl.DeviceIdType.MESH
NT = (((1,), (1,)), ((), ()))
F32 = jnp.float32
BF16 = jnp.bfloat16


def smooth(a):
    g = 0.5 + 0.5 * jnp.tanh(0.5 * a)
    return jnp.maximum(a, 0.0) - jnp.log(jnp.maximum(g, 1.0 - g)), g


def exact_dot(a, b, dims=(((1,), (0,)), ((), ()))):
    return lax.dot_general(a, b, dims, precision=lax.Precision.HIGHEST, preferred_element_type=F32)


def kernel(
    n_trade,
    n_date,
    n_scen,
    cash_hbm,
    dates_hbm,
    sets_hbm,
    slots_hbm,
    lags_hbm,
    limits_hbm,
    cpty_hbm,
    probs_hbm,
    loss_hbm,
    cot_hbm,
    market_ref,
    charge_ref,
    flows_ref,
    cash_ref,
    dates_ref,
    sets_ref,
    slots_ref,
    lags_ref,
    limits_ref,
    cpty_ref,
    probs_ref,
    loss_ref,
    cot_ref,
    fwd,
    fwd_t,
    vals,
    coll,
    gate,
    direct,
    hazard,
    weight,
    member,
    parts_out,
    parts_in,
    set_flows,
    total,
    total_in,
    every,
    trade_rows,
    charge_out,
    charge_in,
    charge_sum,
    charge_far,
    load_sem,
    small_sem,
    halo_sem,
    parts_sem,
    flow_sem,
    total_sem,
    charge_sem,
    far_sem,
    every_sem,
):
    z = lax.axis_index("trade")
    d = lax.axis_index("date")
    c = lax.axis_index("scen")
    n_group = n_date * n_scen
    g = d * n_scen + c
    span, n_u, n_s = market_ref.shape
    n_p = lags_ref.shape[1]
    n_sets = slots_ref.shape[1]
    n_c = probs_ref.shape[1]
    n_n = sets_ref.shape[1]
    n_k = dates_ref.shape[0]
    uq = n_u // n_group
    steps = span + LAGMAX
    first = d * span

    def trade_peer(k):
        return {"trade": lax.rem(z + k, n_trade)}

    def group_peer(k):
        peer = lax.rem(g + k, n_group)
        return {"date": peer // n_scen, "scen": lax.rem(peer, n_scen)}

    others = [(j, k) for j in range(n_trade) for k in range(n_group) if j + k > 0]

    def peer(j, k):
        return {**trade_peer(j), **group_peer(k)}

    def send(src, dst, sems, index, device):
        copy = pltpu.make_async_remote_copy(
            src_ref=src,
            dst_ref=dst,
            send_sem=sems.at[(0,) + index],
            recv_sem=sems.at[(1,) + index],
            device_id=device,
            device_id_type=MESH,
        )
        copy.start()
        return copy

    barrier = pltpu.get_barrier_semaphore()
    for j, k in others:
        pl.semaphore_signal(barrier, inc=1, device_id=peer(j, k), device_id_type=MESH)

    small = [
        pltpu.make_async_copy(src, dst, small_sem.at[i])
        for i, (src, dst) in enumerate(
            (
                (dates_hbm, dates_ref),
                (cash_hbm, cash_ref),
                (sets_hbm, sets_ref),
                (slots_hbm, slots_ref),
                (cpty_hbm, cpty_ref),
                (loss_hbm, loss_ref),
                (cot_hbm, cot_ref),
                (probs_hbm, probs_ref),
                (limits_hbm, limits_ref),
                (lags_hbm, lags_ref),
            )
        )
    ]
    for copy in small:
        copy.start()
    load = pltpu.make_async_copy(market_ref, fwd.at[pl.ds(LAGMAX, span)], load_sem)
    load.start()

    for copy in small:
        copy.wait()

    mine = pl.multiple_of(g * uq, uq)
    u_rows = lax.broadcasted_iota(jnp.int32, (uq, n_n), 0) + g * uq
    grid = jnp.zeros((uq, n_n), F32)
    cash = cash_ref[...].astype(F32)
    moments = dates_ref[...]
    for k in range(n_k):
        grid = jnp.where(u_rows == moments[k : k + 1, :], cash[k : k + 1, :], grid)

    wanted = lax.broadcasted_iota(jnp.int32, (n_sets, n_n), 0) == sets_ref[...]
    slots = slots_ref[...]
    digit = lax.broadcasted_iota(jnp.int32, (8, n_sets), 0)
    digits = jnp.where(digit == 0, slots >> 6, jnp.where(digit == 1, slots & 63, 0))
    found = jnp.dot(digits.astype(F32).astype(BF16), wanted.astype(F32).astype(BF16), preferred_element_type=F32)
    positions = (found[0:1, :] * 64.0 + found[1:2, :]).astype(jnp.int32)
    p_rows = lax.broadcasted_iota(jnp.int32, (n_sets, n_n), 0)
    member[...] = (p_rows == positions).astype(F32).astype(BF16)
    partial = lax.dot_general(grid.astype(BF16), member[...], NT, preferred_element_type=F32)
    for o in range(n_trade):
        parts_out[o] = partial[:, o * n_p : (o + 1) * n_p]

    pl.semaphore_wait(barrier, len(others))
    pending = []
    arrivals = []
    for k in range(1, n_trade):
        to = lax.rem(z + k, n_trade)
        arrivals.append(send(parts_out.at[to], parts_in.at[k], parts_sem, (k,), trade_peer(k)))
    next_date = {"date": lax.rem(d + 1, n_date)}
    halo = send(
        market_ref.at[pl.ds(span - LAGMAX, LAGMAX)], fwd.at[pl.ds(0, LAGMAX)], halo_sem, (), next_date
    )

    named = lax.broadcasted_iota(jnp.int32, (n_c, n_p), 0) == cpty_ref[...]
    named = named.astype(F32)
    loss = loss_ref[...]
    scale_row = lax.broadcasted_iota(jnp.int32, (8, n_c), 0)
    scales = jnp.where(scale_row == 0, loss, jnp.where(scale_row == 1, loss * cot_ref[...], 0.0))
    scales = exact_dot(scales, named)
    paths = float(n_s * n_scen)
    hazard[...] = exact_dot(probs_ref[...], named)
    weight[...] = hazard[...] * (scales[1:2, :] / paths)

    u_col = lax.broadcasted_iota(jnp.int32, (n_u, n_s), 0)

    def mask_dates(t, shown):
        later = (u_col > first + (t - LAGMAX)).astype(F32) * shown
        block = fwd[t] * later.astype(BF16)
        fwd[t] = block
        fwd_t[t] = block.T

    load.wait()

    def mask_step(i, carry):
        for b in range(STEP):
            mask_dates(LAGMAX + i * STEP + b, 1.0)
        return carry

    lax.fori_loop(0, span // STEP, mask_step, 0)

    for copy in arrivals:
        copy.wait_recv()
    pending += arrivals
    mine_sum = parts_out[z]
    for k in range(1, n_trade):
        mine_sum = mine_sum + parts_in[k]
    set_flows[pl.ds(mine, uq), :] = mine_sum.astype(BF16)
    arrivals = []
    for k in range(1, n_group):
        block = set_flows.at[pl.ds(mine, uq)]
        arrivals.append(send(block, block, flow_sem, (k,), group_peer(k)))

    halo.wait()
    after_first = jnp.where(d > 0, 1.0, 0.0).astype(F32)
    for b in range(LAGMAX):
        mask_dates(b, after_first)
    for copy in arrivals:
        copy.wait_recv()
    pending += arrivals

    flows = set_flows[...]
    limits = limits_ref[...] * RATE

    lags = lags_ref[...]
    lags16 = lags.astype(F32).astype(BF16)

    def by_lag(which, rows):
        out = rows[0]
        for lag in range(1, LAGMAX + 1):
            out = jnp.where(which == which.dtype.type(lag), rows[lag], out)
        return out

    def value_block(i, shown=None):
        for b in range(LAGMAX):
            t = i * LAGMAX + b
            v = jnp.dot(fwd_t[t], flows, preferred_element_type=F32) * RATE
            amount, slope = smooth(v - limits)
            if shown is not None:
                amount, slope = amount * shown, slope * shown
            vals[t] = v
            coll[t] = amount
            gate[t] = slope.astype(BF16)

    def exposure_block(i, acc):
        for b in range(LAGMAX):
            t = i * LAGMAX + b
            margin = vals[t] - by_lag(lags, [coll[t - lag] for lag in range(LAGMAX + 1)])
            amount, slope = smooth(margin)
            own = pl.ds(t - LAGMAX, 1)
            acc = acc + jnp.sum(amount.reshape(-1, 8, n_p), axis=0) * hazard[own, :]
            direct[t] = (slope * weight[own, :]).astype(BF16)
        return acc

    def grad_block(i):
        out = None
        for b in range(LAGMAX):
            t = i * LAGMAX + b
            later = by_lag(lags16, [direct[t + lag] for lag in range(LAGMAX + 1)])
            block = direct[t] - later * gate[t]
            term = jnp.dot(fwd[t], block, preferred_element_type=F32)
            out = term if out is None else out + term
        total[...] += out

    for b in range(LAGMAX):
        direct[b] = jnp.zeros((n_s, n_p), BF16)
        direct[steps + b] = jnp.zeros((n_s, n_p), BF16)
    total[...] = jnp.zeros((n_u, n_p), F32)

    last = steps // LAGMAX - 1
    value_block(0, after_first)
    value_block(1)
    acc = exposure_block(1, jnp.zeros((8, n_p), F32))
    value_block(2)

    def block_step(i, acc):
        grad_block(i - 3)
        acc = exposure_block(i - 1, acc)
        value_block(i)
        return acc

    acc = lax.fori_loop(3, last + 1, block_step, acc)
    acc = exposure_block(last, acc)
    terms = jnp.sum(acc, axis=0, keepdims=True) * (scales[0:1, :] * (1.0 / (RATE * paths)))
    charge_out[...] = exact_dot(jnp.broadcast_to(terms, (8, n_p)), named, NT)
    charges = []
    for k in range(1, n_group):
        charges.append(send(charge_out, charge_in.at[k], charge_sem, (k,), group_peer(k)))
    for i in range(last - 2, last + 1):
        grad_block(i)

    arrivals = []
    for k in range(1, n_group):
        theirs = pl.multiple_of(lax.rem(g + k, n_group) * uq, uq)
        arrivals.append(
            send(total.at[pl.ds(theirs, uq)], total_in.at[k], total_sem, (k,), group_peer(k))
        )

    for copy in charges:
        copy.wait_recv()
    pending += charges
    group_charge = charge_out[...]
    for k in range(1, n_group):
        group_charge = group_charge + charge_in[k]
    charge_sum[...] = group_charge
    charges = []
    for k in range(1, n_trade):
        charges.append(send(charge_sum, charge_far.at[k], far_sem, (k,), trade_peer(k)))

    for copy in arrivals:
        copy.wait_recv()
    pending += arrivals
    mine_sum = total[pl.ds(mine, uq), :]
    for k in range(1, n_group):
        mine_sum = mine_sum + total_in[k]
    every[z, pl.ds(mine, uq), :] = mine_sum.astype(BF16)

    block = every.at[z, pl.ds(mine, uq)]
    final = [send(block, block, every_sem, (j, k), peer(j, k)) for j, k in others]
    for copy in charges:
        copy.wait_recv()
    pending += charges
    group_charge = charge_sum[...]
    for k in range(1, n_trade):
        group_charge = group_charge + charge_far[k]
    charge_ref[...] = group_charge[0:1, :]

    for copy in final:
        copy.wait_recv()
    pending += final
    rows = jnp.zeros((n_u, n_n), F32)
    for o in range(n_trade):
        rows = rows + jnp.dot(every[o], member[o * n_p : (o + 1) * n_p, :], preferred_element_type=F32)
    trade_rows[...] = rows

    def pick_step(i, out):
        base = pl.multiple_of(i * 8, 8)
        rows = trade_rows[pl.ds(base, 8), :]
        for b in range(8):
            out = jnp.where(moments == base + b, rows[b : b + 1, :], out)
        return out

    flows_ref[...] = lax.fori_loop(0, n_u // 8, pick_step, jnp.zeros((n_k, n_n), F32))
    for copy in pending:
        copy.wait_send()


def write_out(charge_ref, flows_ref, charge_out, flows_out, sems):
    copies = [
        pltpu.make_async_copy(flows_ref, flows_out, sems.at[0]),
        pltpu.make_async_copy(charge_ref, charge_out, sems.at[1]),
    ]
    for copy in copies:
        copy.start()
    for copy in copies:
        copy.wait()


def per_device(
    cash_flows,
    coupon_dates,
    trade_sets,
    set_slots,
    set_lags,
    thresholds,
    set_cpty,
    discounts,
    default_probs,
    loss_given,
    cva_cotangent,
):
    n_trade, n_date, n_scen = (lax.axis_size(a) for a in ("trade", "date", "scen"))
    n_group = n_date * n_scen
    n_n, n_k = cash_flows.shape
    span, n_u, n_s = discounts.shape
    n_p = set_lags.shape[0]
    n_sets = set_slots.shape[0]
    n_c = loss_given.shape[0]
    uq = n_u // n_group
    steps = span + LAGMAX
    vmem = pl.BlockSpec(memory_space=pltpu.VMEM)
    dma = pltpu.SemaphoreType.DMA
    charge, flow_grads = pl.pallas_call(
        functools.partial(kernel, n_trade, n_date, n_scen),
        out_shape=(
            jax.ShapeDtypeStruct((1, n_c), F32),
            jax.ShapeDtypeStruct((n_k, n_n), F32),
        ),
        in_specs=[pl.BlockSpec(memory_space=pltpu.HBM)] * 11,
        out_specs=(vmem, vmem),
        scratch_shapes=[
            pltpu.VMEM((n_k, n_n), cash_flows.dtype),
            pltpu.VMEM((n_k, n_n), jnp.int32),
            pltpu.VMEM((1, n_n), jnp.int32),
            pltpu.VMEM((1, n_sets), jnp.int32),
            pltpu.VMEM((1, n_p), jnp.int32),
            pltpu.VMEM((1, n_p), F32),
            pltpu.VMEM((1, n_p), jnp.int32),
            pltpu.VMEM((span, n_c), F32),
            pltpu.VMEM((1, n_c), F32),
            pltpu.VMEM((1, n_c), F32),
            pltpu.VMEM((steps, n_u, n_s), BF16),
            pltpu.VMEM((steps, n_s, n_u), BF16),
            pltpu.VMEM((steps, n_s, n_p), F32),
            pltpu.VMEM((steps, n_s, n_p), F32),
            pltpu.VMEM((steps, n_s, n_p), BF16),
            pltpu.VMEM((steps + LAGMAX, n_s, n_p), BF16),
            pltpu.VMEM((span, n_p), F32),
            pltpu.VMEM((span, n_p), F32),
            pltpu.VMEM((n_sets, n_n), BF16),
            pltpu.VMEM((n_trade, uq, n_p), F32),
            pltpu.VMEM((n_trade, uq, n_p), F32),
            pltpu.VMEM((n_u, n_p), BF16),
            pltpu.VMEM((n_u, n_p), F32),
            pltpu.VMEM((n_group, uq, n_p), F32),
            pltpu.VMEM((n_trade, n_u, n_p), BF16),
            pltpu.VMEM((n_u, n_n), F32),
            pltpu.VMEM((8, n_c), F32),
            pltpu.VMEM((n_group, 8, n_c), F32),
            pltpu.VMEM((8, n_c), F32),
            pltpu.VMEM((n_trade, 8, n_c), F32),
            dma,
            dma((10,)),
            dma((2,)),
            dma((2, n_trade)),
            dma((2, n_group)),
            dma((2, n_group)),
            dma((2, n_group)),
            dma((2, n_trade)),
            dma((2, n_trade, n_group)),
        ],
        compiler_params=pltpu.CompilerParams(
            collective_id=0, has_side_effects=True, vmem_limit_bytes=48 * 1024 * 1024
        ),
    )(
        *(
            pltpu.with_memory_space_constraint(a, pltpu.HBM)
            for a in (
                cash_flows.T,
                coupon_dates.T,
                trade_sets.reshape(1, -1),
                set_slots.reshape(1, -1),
                set_lags.reshape(1, -1),
                thresholds.reshape(1, -1),
                set_cpty.reshape(1, -1),
                default_probs.T,
                loss_given.reshape(1, -1),
                cva_cotangent.reshape(1, -1),
                discounts,
            )
        )
    )
    return charge.reshape(-1), flow_grads.T


def solution(mesh):
    in_specs = (
        P("trade", None),
        P("trade", None),
        P("trade"),
        P(),
        P("trade"),
        P("trade"),
        P("trade"),
        P("date", None, ("groups", "scen")),
        P(None, "date"),
        P(),
        P(),
    )
    out_specs = (P("groups"), P(("groups", "trade"), None))
    return jax.shard_map(
        per_device, mesh=mesh, in_specs=in_specs, out_specs=out_specs, check_vma=False
    )
```

```python
import functools

import jax
import jax.numpy as jnp
from jax import lax
from jax.experimental import pallas as pl
from jax.experimental.pallas import tpu as pltpu
from jax.sharding import PartitionSpec as P

LAGMAX = 4
RATE = 10.0
SLAB = 32
LOG2 = 0.6931471805599453
STEP = 4
MESH = pl.DeviceIdType.MESH
NT = (((1,), (1,)), ((), ()))
F32 = jnp.float32
BF16 = jnp.bfloat16


def exact_dot(a, b, dims=(((1,), (0,)), ((), ()))):
    return lax.dot_general(a, b, dims, precision=lax.Precision.HIGHEST, preferred_element_type=F32)


def kernel(
    n_trade,
    n_date,
    n_scen,
    cash_hbm,
    dates_hbm,
    sets_hbm,
    slots_hbm,
    lags_hbm,
    limits_hbm,
    cpty_hbm,
    probs_hbm,
    loss_hbm,
    cot_hbm,
    market_ref,
    charge_ref,
    flows_ref,
    cash_ref,
    dates_ref,
    sets_ref,
    slots_ref,
    lags_ref,
    limits_ref,
    cpty_ref,
    probs_ref,
    loss_ref,
    cot_ref,
    fwd,
    fwd_t,
    vals,
    coll,
    gate,
    direct,
    hazard,
    weight,
    member,
    parts,
    parts_out,
    parts_in,
    total,
    total_in,
    every,
    trade_rows,
    charge_out,
    charge_in,
    charge_sum,
    charge_far,
    load_sem,
    small_sem,
    halo_sem,
    parts_sem,
    total_sem,
    charge_sem,
    far_sem,
    every_sem,
):
    z = lax.axis_index("trade")
    d = lax.axis_index("date")
    c = lax.axis_index("scen")
    n_group = n_date * n_scen
    g = d * n_scen + c
    span, n_u, n_s = market_ref.shape
    n_p = lags_ref.shape[1]
    n_sets = slots_ref.shape[1]
    n_c = probs_ref.shape[1]
    n_n = sets_ref.shape[1]
    n_k = dates_ref.shape[0]
    uq = n_u // n_group
    steps = span + LAGMAX
    first = d * span

    def trade_peer(k):
        return {"trade": lax.rem(z + k, n_trade)}

    def group_peer(k):
        peer = lax.rem(g + k, n_group)
        return {"date": peer // n_scen, "scen": lax.rem(peer, n_scen)}

    others = [(j, k) for j in range(n_trade) for k in range(n_group) if j + k > 0]

    near = [(j, k) for j, k in others if j * k == 0]

    def peer(j, k):
        return {**trade_peer(j), **group_peer(k)}

    def send(src, dst, sems, index, device):
        copy = pltpu.make_async_remote_copy(
            src_ref=src,
            dst_ref=dst,
            send_sem=sems.at[(0,) + index],
            recv_sem=sems.at[(1,) + index],
            device_id=device,
            device_id_type=MESH,
        )
        copy.start()
        return copy

    barrier = pltpu.get_barrier_semaphore()
    for j, k in others:
        pl.semaphore_signal(barrier, inc=1, device_id=peer(j, k), device_id_type=MESH)

    small = [
        pltpu.make_async_copy(src, dst, small_sem.at[i])
        for i, (src, dst) in enumerate(
            (
                (dates_hbm, dates_ref),
                (cash_hbm, cash_ref),
                (sets_hbm, sets_ref),
                (slots_hbm, slots_ref),
                (cpty_hbm, cpty_ref),
                (loss_hbm, loss_ref),
                (cot_hbm, cot_ref),
                (probs_hbm, probs_ref),
                (limits_hbm, limits_ref),
                (lags_hbm, lags_ref),
            )
        )
    ]
    for copy in small:
        copy.start()
    load = pltpu.make_async_copy(market_ref, fwd.at[pl.ds(LAGMAX, span)], load_sem)
    load.start()

    for copy in small:
        copy.wait()

    mine = pl.multiple_of(g * uq, uq)
    u_rows = lax.broadcasted_iota(jnp.int32, (n_u, n_n), 0)
    grid = jnp.zeros((n_u, n_n), F32)
    cash = cash_ref[...].astype(F32)
    moments = dates_ref[...]
    for k in range(n_k):
        grid = jnp.where(u_rows == moments[k : k + 1, :], cash[k : k + 1, :], grid)

    wanted = lax.broadcasted_iota(jnp.int32, (n_sets, n_n), 0) == sets_ref[...]
    slots = slots_ref[...]
    digit = lax.broadcasted_iota(jnp.int32, (8, n_sets), 0)
    digits = jnp.where(digit == 0, slots >> 6, jnp.where(digit == 1, slots & 63, 0))
    found = jnp.dot(digits.astype(F32).astype(BF16), wanted.astype(F32).astype(BF16), preferred_element_type=F32)
    positions = (found[0:1, :] * 64.0 + found[1:2, :]).astype(jnp.int32)
    p_rows = lax.broadcasted_iota(jnp.int32, (n_sets, n_n), 0)
    member[...] = (p_rows == positions).astype(F32).astype(BF16)
    partial = lax.dot_general(grid.astype(BF16), member[...], NT, preferred_element_type=F32)
    for o in range(n_trade):
        own_part = partial[:, o * n_p : (o + 1) * n_p]
        parts[o] = own_part
        parts_out[o] = own_part.astype(BF16)

    pl.semaphore_wait(barrier, len(others))
    pending = []
    arrivals = []
    for k in range(1, n_trade):
        to = lax.rem(z + k, n_trade)
        arrivals.append(send(parts_out.at[to], parts_in.at[k], parts_sem, (k,), trade_peer(k)))
    next_date = {"date": lax.rem(d + 1, n_date)}
    halo = send(
        market_ref.at[pl.ds(span - LAGMAX, LAGMAX)], fwd.at[pl.ds(0, LAGMAX)], halo_sem, (), next_date
    )

    named = lax.broadcasted_iota(jnp.int32, (n_c, n_p), 0) == cpty_ref[...]
    named = named.astype(F32)
    loss = loss_ref[...]
    scale_row = lax.broadcasted_iota(jnp.int32, (8, n_c), 0)
    scales = jnp.where(scale_row == 0, loss, jnp.where(scale_row == 1, loss * cot_ref[...], 0.0))
    scales = exact_dot(scales, named)
    paths = float(n_s * n_scen)
    hazard[...] = exact_dot(probs_ref[...], named)
    weight[...] = hazard[...] * (scales[1:2, :] * (0.5 / paths))

    u_col = lax.broadcasted_iota(jnp.int32, (n_u, n_s), 0)

    def mask_dates(t, shown):
        later = (u_col > first + (t - LAGMAX)).astype(F32) * shown
        block = fwd[t] * later.astype(BF16)
        fwd[t] = block
        fwd_t[t] = block.T

    load.wait()

    def mask_step(i, carry):
        for b in range(STEP):
            mask_dates(LAGMAX + i * STEP + b, 1.0)
        return carry

    lax.fori_loop(0, span // STEP, mask_step, 0)

    for copy in arrivals:
        copy.wait_recv()
    pending += arrivals
    flow_sum = parts[z]
    for k in range(1, n_trade):
        flow_sum = flow_sum + parts_in[k].astype(F32)
    flows = flow_sum.astype(BF16)

    halo.wait()
    after_first = jnp.where(d > 0, 1.0, 0.0).astype(F32)
    for b in range(LAGMAX):
        mask_dates(b, after_first)
    limits = limits_ref[...] * (0.5 * RATE)

    lags = lags_ref[...]
    lags16 = lags.astype(F32).astype(BF16)

    def by_lag(which, rows):
        out = rows[0]
        for lag in range(1, LAGMAX + 1):
            out = jnp.where(which == which.dtype.type(lag), rows[lag], out)
        return out

    def value_block(i, shown=None):
        base = pl.multiple_of(i * LAGMAX, LAGMAX)
        rows = fwd_t[pl.ds(base, LAGMAX)].reshape(LAGMAX * n_s, n_u)
        v = jnp.dot(rows, flows, preferred_element_type=F32) * (0.5 * RATE)
        a = v - limits
        half = 0.5 * jnp.tanh(a)
        amount = jnp.maximum(a, 0.0) - 0.5 * jnp.log(0.5 + jnp.abs(half))
        slope = 0.5 + half
        if shown is not None:
            amount, slope = amount * shown, slope * shown
        shape = (LAGMAX, n_s, n_p)
        vals[pl.ds(base, LAGMAX)] = v.reshape(shape)
        coll[pl.ds(base, LAGMAX)] = amount.reshape(shape)
        gate[pl.ds(base, LAGMAX)] = slope.astype(BF16).reshape(shape)

    def exposure_block(i, acc):
        for b in range(LAGMAX):
            t = i * LAGMAX + b
            own = pl.ds(t - LAGMAX, 1)
            scale = weight[own, :]
            gain = jnp.zeros((8, n_p), F32)
            for low in range(0, n_s, SLAB):
                at = pl.ds(low, SLAB)
                margin = vals[t, at] - by_lag(lags, [coll[t - lag, at] for lag in range(LAGMAX + 1)])
                turn = jnp.tanh(margin)
                direct[t, at] = (scale + scale * turn).astype(BF16)
                factors = 1.0 + jnp.abs(turn)
                product = factors[0:8]
                for m in range(8, SLAB, 8):
                    product = product * factors[m : m + 8]
                above = jnp.sum(jnp.maximum(margin, 0.0).reshape(SLAB // 8, 8, n_p), axis=0)
                gain = gain + (above - 0.5 * jnp.log(product))
            acc = acc + (gain + 0.5 * LOG2 * (n_s // 8)) * hazard[own, :]
        return acc

    def grad_block(i):
        blocks, rows = [], []
        for b in range(LAGMAX):
            t = i * LAGMAX + b
            for low in range(0, n_s, SLAB):
                at = pl.ds(low, SLAB)
                later = by_lag(lags16, [direct[t + lag, at] for lag in range(LAGMAX + 1)])
                blocks.append(direct[t, at] - later * gate[t, at])
            rows.append(fwd[t])
        total[...] += jnp.dot(
            jnp.concatenate(rows, axis=1),
            jnp.concatenate(blocks, axis=0),
            preferred_element_type=F32,
        )

    for b in range(LAGMAX):
        direct[b] = jnp.zeros((n_s, n_p), BF16)
        direct[steps + b] = jnp.zeros((n_s, n_p), BF16)
    total[...] = jnp.zeros((n_u, n_p), F32)

    last = steps // LAGMAX - 1
    value_block(0, after_first)
    value_block(1)
    acc = exposure_block(1, jnp.zeros((8, n_p), F32))
    value_block(2)

    def block_step(i, acc):
        grad_block(i - 3)
        acc = exposure_block(i - 1, acc)
        value_block(i)
        return acc

    acc = lax.fori_loop(3, last + 1, block_step, acc)
    acc = exposure_block(last, acc)
    terms = jnp.sum(acc, axis=0, keepdims=True) * (scales[0:1, :] * (2.0 / (RATE * paths)))
    charge_out[...] = exact_dot(jnp.broadcast_to(terms, (8, n_p)), named, NT)
    charges = []
    for k in range(1, n_group):
        charges.append(send(charge_out, charge_in.at[k], charge_sem, (k,), group_peer(k)))
    for i in range(last - 2, last + 1):
        grad_block(i)

    arrivals = []
    for k in range(1, n_group):
        theirs = pl.multiple_of(lax.rem(g + k, n_group) * uq, uq)
        arrivals.append(
            send(total.at[pl.ds(theirs, uq)], total_in.at[k], total_sem, (k,), group_peer(k))
        )

    for copy in charges:
        copy.wait_recv()
    pending += charges
    group_charge = charge_out[...]
    for k in range(1, n_group):
        group_charge = group_charge + charge_in[k]
    charge_sum[...] = group_charge
    charges = []
    for k in range(1, n_trade):
        charges.append(send(charge_sum, charge_far.at[k], far_sem, (k,), trade_peer(k)))

    for copy in arrivals:
        copy.wait_recv()
    pending += arrivals
    mine_sum = total[pl.ds(mine, uq), :]
    for k in range(1, n_group):
        mine_sum = mine_sum + total_in[k]
    every[z, pl.ds(mine, uq), :] = mine_sum.astype(BF16)

    block = every.at[z, pl.ds(mine, uq)]
    final = [send(block, block, every_sem, (j, k), peer(j, k)) for j, k in sorted(others, key=lambda p: (p[0], -p[1]))]
    for copy in charges:
        copy.wait_recv()
    pending += charges
    group_charge = charge_sum[...]
    for k in range(1, n_trade):
        group_charge = group_charge + charge_far[k]
    charge_ref[...] = group_charge[0:1, :]

    for copy in final:
        copy.wait_recv()
    pending += final
    rows = jnp.zeros((n_u, n_n), F32)
    for o in range(n_trade):
        rows = rows + jnp.dot(every[o], member[o * n_p : (o + 1) * n_p, :], preferred_element_type=F32)
    trade_rows[...] = rows

    def pick_step(i, out):
        base = pl.multiple_of(i * 8, 8)
        rows = trade_rows[pl.ds(base, 8), :]
        for b in range(8):
            out = jnp.where(moments == base + b, rows[b : b + 1, :], out)
        return out

    flows_ref[...] = lax.fori_loop(0, n_u // 8, pick_step, jnp.zeros((n_k, n_n), F32))
    for copy in pending:
        copy.wait_send()


def write_out(charge_ref, flows_ref, charge_out, flows_out, sems):
    copies = [
        pltpu.make_async_copy(flows_ref, flows_out, sems.at[0]),
        pltpu.make_async_copy(charge_ref, charge_out, sems.at[1]),
    ]
    for copy in copies:
        copy.start()
    for copy in copies:
        copy.wait()


def per_device(
    cash_flows,
    coupon_dates,
    trade_sets,
    set_slots,
    set_lags,
    thresholds,
    set_cpty,
    discounts,
    default_probs,
    loss_given,
    cva_cotangent,
):
    n_trade, n_date, n_scen = (lax.axis_size(a) for a in ("trade", "date", "scen"))
    n_group = n_date * n_scen
    n_n, n_k = cash_flows.shape
    span, n_u, n_s = discounts.shape
    n_p = set_lags.shape[0]
    n_sets = set_slots.shape[0]
    n_c = loss_given.shape[0]
    uq = n_u // n_group
    steps = span + LAGMAX
    vmem = pl.BlockSpec(memory_space=pltpu.VMEM)
    dma = pltpu.SemaphoreType.DMA
    charge, flow_grads = pl.pallas_call(
        functools.partial(kernel, n_trade, n_date, n_scen),
        out_shape=(
            jax.ShapeDtypeStruct((1, n_c), F32),
            jax.ShapeDtypeStruct((n_k, n_n), F32),
        ),
        in_specs=[pl.BlockSpec(memory_space=pltpu.HBM)] * 11,
        out_specs=(vmem, vmem),
        scratch_shapes=[
            pltpu.VMEM((n_k, n_n), cash_flows.dtype),
            pltpu.VMEM((n_k, n_n), jnp.int32),
            pltpu.VMEM((1, n_n), jnp.int32),
            pltpu.VMEM((1, n_sets), jnp.int32),
            pltpu.VMEM((1, n_p), jnp.int32),
            pltpu.VMEM((1, n_p), F32),
            pltpu.VMEM((1, n_p), jnp.int32),
            pltpu.VMEM((span, n_c), F32),
            pltpu.VMEM((1, n_c), F32),
            pltpu.VMEM((1, n_c), F32),
            pltpu.VMEM((steps, n_u, n_s), BF16),
            pltpu.VMEM((steps, n_s, n_u), BF16),
            pltpu.VMEM((steps, n_s, n_p), F32),
            pltpu.VMEM((steps, n_s, n_p), F32),
            pltpu.VMEM((steps, n_s, n_p), BF16),
            pltpu.VMEM((steps + LAGMAX, n_s, n_p), BF16),
            pltpu.VMEM((span, n_p), F32),
            pltpu.VMEM((span, n_p), F32),
            pltpu.VMEM((n_sets, n_n), BF16),
            pltpu.VMEM((n_trade, n_u, n_p), F32),
            pltpu.VMEM((n_trade, n_u, n_p), BF16),
            pltpu.VMEM((n_trade, n_u, n_p), BF16),
            pltpu.VMEM((n_u, n_p), F32),
            pltpu.VMEM((n_group, uq, n_p), F32),
            pltpu.VMEM((n_trade, n_u, n_p), BF16),
            pltpu.VMEM((n_u, n_n), F32),
            pltpu.VMEM((8, n_c), F32),
            pltpu.VMEM((n_group, 8, n_c), F32),
            pltpu.VMEM((8, n_c), F32),
            pltpu.VMEM((n_trade, 8, n_c), F32),
            dma,
            dma((10,)),
            dma((2,)),
            dma((2, n_trade)),
            dma((2, n_group)),
            dma((2, n_group)),
            dma((2, n_trade)),
            dma((2, n_trade, n_group)),
        ],
        compiler_params=pltpu.CompilerParams(
            collective_id=0, has_side_effects=True, vmem_limit_bytes=48 * 1024 * 1024
        ),
    )(
        *(
            pltpu.with_memory_space_constraint(a, pltpu.HBM)
            for a in (
                cash_flows.T,
                coupon_dates.T,
                trade_sets.reshape(1, -1),
                set_slots.reshape(1, -1),
                set_lags.reshape(1, -1),
                thresholds.reshape(1, -1),
                set_cpty.reshape(1, -1),
                default_probs.T,
                loss_given.reshape(1, -1),
                cva_cotangent.reshape(1, -1),
                discounts,
            )
        )
    )
    return charge.reshape(-1), flow_grads.T


def solution(mesh):
    in_specs = (
        P("trade", None),
        P("trade", None),
        P("trade"),
        P(),
        P("trade"),
        P("trade"),
        P("trade"),
        P("date", None, ("groups", "scen")),
        P(None, "date"),
        P(),
        P(),
    )
    out_specs = (P("groups"), P(("groups", "trade"), None))
    return jax.shard_map(
        per_device, mesh=mesh, in_specs=in_specs, out_specs=out_specs, check_vma=False
    )
```

```python
import functools

import jax
import jax.numpy as jnp
from jax import lax
from jax.experimental import pallas as pl
from jax.experimental.pallas import tpu as pltpu
from jax.sharding import PartitionSpec as P

LAGMAX = 4
RATE = 10.0
SLAB = 32
LOG2 = 0.6931471805599453
STEP = 4
MESH = pl.DeviceIdType.MESH
NT = (((1,), (1,)), ((), ()))
F32 = jnp.float32
BF16 = jnp.bfloat16


def exact_dot(a, b, dims=(((1,), (0,)), ((), ()))):
    return lax.dot_general(a, b, dims, precision=lax.Precision.HIGHEST, preferred_element_type=F32)


def kernel(
    n_trade,
    n_date,
    n_scen,
    cash_hbm,
    dates_hbm,
    sets_hbm,
    slots_hbm,
    lags_hbm,
    limits_hbm,
    cpty_hbm,
    probs_hbm,
    loss_hbm,
    cot_hbm,
    market_ref,
    charge_ref,
    flows_ref,
    cash_ref,
    dates_ref,
    sets_ref,
    slots_ref,
    lags_ref,
    limits_ref,
    cpty_ref,
    probs_ref,
    loss_ref,
    cot_ref,
    fwd,
    fwd_t,
    vals,
    coll,
    gate,
    direct,
    hazard,
    weight,
    member,
    parts_out,
    parts_in,
    set_flows,
    total,
    total_in,
    every,
    trade_rows,
    charge_out,
    charge_in,
    charge_sum,
    charge_far,
    load_sem,
    small_sem,
    halo_sem,
    parts_sem,
    flow_sem,
    total_sem,
    charge_sem,
    far_sem,
    every_sem,
):
    z = lax.axis_index("trade")
    d = lax.axis_index("date")
    c = lax.axis_index("scen")
    n_group = n_date * n_scen
    g = d * n_scen + c
    span, n_u, n_s = market_ref.shape
    n_p = lags_ref.shape[1]
    n_sets = slots_ref.shape[1]
    n_c = probs_ref.shape[1]
    n_n = sets_ref.shape[1]
    n_k = dates_ref.shape[0]
    uq = n_u // n_group
    steps = span + LAGMAX
    first = d * span

    def trade_peer(k):
        return {"trade": lax.rem(z + k, n_trade)}

    def group_peer(k):
        peer = lax.rem(g + k, n_group)
        return {"date": peer // n_scen, "scen": lax.rem(peer, n_scen)}

    others = [(j, k) for j in range(n_trade) for k in range(n_group) if j + k > 0]

    near = [(j, k) for j, k in others if j * k == 0]

    def peer(j, k):
        return {**trade_peer(j), **group_peer(k)}

    def send(src, dst, sems, index, device):
        copy = pltpu.make_async_remote_copy(
            src_ref=src,
            dst_ref=dst,
            send_sem=sems.at[(0,) + index],
            recv_sem=sems.at[(1,) + index],
            device_id=device,
            device_id_type=MESH,
        )
        copy.start()
        return copy

    barrier = pltpu.get_barrier_semaphore()
    for j, k in others:
        pl.semaphore_signal(barrier, inc=1, device_id=peer(j, k), device_id_type=MESH)

    small = [
        pltpu.make_async_copy(src, dst, small_sem.at[i])
        for i, (src, dst) in enumerate(
            (
                (dates_hbm, dates_ref),
                (cash_hbm, cash_ref),
                (sets_hbm, sets_ref),
                (slots_hbm, slots_ref),
                (cpty_hbm, cpty_ref),
                (loss_hbm, loss_ref),
                (cot_hbm, cot_ref),
                (probs_hbm, probs_ref),
                (limits_hbm, limits_ref),
                (lags_hbm, lags_ref),
            )
        )
    ]
    for copy in small:
        copy.start()
    load = pltpu.make_async_copy(market_ref, fwd.at[pl.ds(LAGMAX, span)], load_sem)
    load.start()

    for copy in small:
        copy.wait()

    mine = pl.multiple_of(g * uq, uq)
    u_rows = lax.broadcasted_iota(jnp.int32, (uq, n_n), 0) + g * uq
    grid = jnp.zeros((uq, n_n), F32)
    cash = cash_ref[...].astype(F32)
    moments = dates_ref[...]
    for k in range(n_k):
        grid = jnp.where(u_rows == moments[k : k + 1, :], cash[k : k + 1, :], grid)

    wanted = lax.broadcasted_iota(jnp.int32, (n_sets, n_n), 0) == sets_ref[...]
    slots = slots_ref[...]
    digit = lax.broadcasted_iota(jnp.int32, (8, n_sets), 0)
    digits = jnp.where(digit == 0, slots >> 6, jnp.where(digit == 1, slots & 63, 0))
    found = jnp.dot(digits.astype(F32).astype(BF16), wanted.astype(F32).astype(BF16), preferred_element_type=F32)
    positions = (found[0:1, :] * 64.0 + found[1:2, :]).astype(jnp.int32)
    p_rows = lax.broadcasted_iota(jnp.int32, (n_sets, n_n), 0)
    member[...] = (p_rows == positions).astype(F32).astype(BF16)
    partial = lax.dot_general(grid.astype(BF16), member[...], NT, preferred_element_type=F32)
    for o in range(n_trade):
        parts_out[o] = partial[:, o * n_p : (o + 1) * n_p]

    pl.semaphore_wait(barrier, len(others))
    pending = []
    arrivals = []
    for k in range(1, n_trade):
        to = lax.rem(z + k, n_trade)
        arrivals.append(send(parts_out.at[to], parts_in.at[k], parts_sem, (k,), trade_peer(k)))
    next_date = {"date": lax.rem(d + 1, n_date)}
    halo = send(
        market_ref.at[pl.ds(span - LAGMAX, LAGMAX)], fwd.at[pl.ds(0, LAGMAX)], halo_sem, (), next_date
    )

    named = lax.broadcasted_iota(jnp.int32, (n_c, n_p), 0) == cpty_ref[...]
    named = named.astype(F32)
    loss = loss_ref[...]
    scale_row = lax.broadcasted_iota(jnp.int32, (8, n_c), 0)
    scales = jnp.where(scale_row == 0, loss, jnp.where(scale_row == 1, loss * cot_ref[...], 0.0))
    scales = exact_dot(scales, named)
    paths = float(n_s * n_scen)
    hazard[...] = exact_dot(probs_ref[...], named)
    weight[...] = hazard[...] * (scales[1:2, :] * (0.5 / paths))

    u_col = lax.broadcasted_iota(jnp.int32, (n_u, n_s), 0)

    def mask_dates(t, shown):
        later = (u_col > first + (t - LAGMAX)).astype(F32) * shown
        block = fwd[t] * later.astype(BF16)
        fwd[t] = block
        fwd_t[t] = block.T

    load.wait()

    def mask_step(i, carry):
        for b in range(STEP):
            mask_dates(LAGMAX + i * STEP + b, 1.0)
        return carry

    lax.fori_loop(0, span // STEP, mask_step, 0)

    for copy in arrivals:
        copy.wait_recv()
    pending += arrivals
    mine_sum = parts_out[z]
    for k in range(1, n_trade):
        mine_sum = mine_sum + parts_in[k]
    set_flows[pl.ds(mine, uq), :] = mine_sum.astype(BF16)
    arrivals = []
    for k in range(1, n_group):
        block = set_flows.at[pl.ds(mine, uq)]
        arrivals.append(send(block, block, flow_sem, (k,), group_peer(k)))

    halo.wait()
    after_first = jnp.where(d > 0, 1.0, 0.0).astype(F32)
    for b in range(LAGMAX):
        mask_dates(b, after_first)
    for copy in arrivals:
        copy.wait_recv()
    pending += arrivals

    flows = set_flows[...]
    limits = limits_ref[...] * (0.5 * RATE)

    lags = lags_ref[...]
    lags16 = lags.astype(F32).astype(BF16)

    def by_lag(which, rows):
        out = rows[0]
        for lag in range(1, LAGMAX + 1):
            out = jnp.where(which == which.dtype.type(lag), rows[lag], out)
        return out

    def value_block(i, shown=None):
        base = pl.multiple_of(i * LAGMAX, LAGMAX)
        rows = fwd_t[pl.ds(base, LAGMAX)].reshape(LAGMAX * n_s, n_u)
        v = jnp.dot(rows, flows, preferred_element_type=F32) * (0.5 * RATE)
        a = v - limits
        half = 0.5 * jnp.tanh(a)
        amount = jnp.maximum(a, 0.0) - 0.5 * jnp.log(0.5 + jnp.abs(half))
        slope = 0.5 + half
        if shown is not None:
            amount, slope = amount * shown, slope * shown
        shape = (LAGMAX, n_s, n_p)
        vals[pl.ds(base, LAGMAX)] = v.reshape(shape)
        coll[pl.ds(base, LAGMAX)] = amount.reshape(shape)
        gate[pl.ds(base, LAGMAX)] = slope.astype(BF16).reshape(shape)

    def exposure_block(i, acc):
        for b in range(LAGMAX):
            t = i * LAGMAX + b
            own = pl.ds(t - LAGMAX, 1)
            scale = weight[own, :]
            gain = jnp.zeros((8, n_p), F32)
            for low in range(0, n_s, SLAB):
                at = pl.ds(low, SLAB)
                margin = vals[t, at] - by_lag(lags, [coll[t - lag, at] for lag in range(LAGMAX + 1)])
                turn = jnp.tanh(margin)
                direct[t, at] = (scale + scale * turn).astype(BF16)
                factors = 1.0 + jnp.abs(turn)
                product = factors[0:8]
                for m in range(8, SLAB, 8):
                    product = product * factors[m : m + 8]
                above = jnp.sum(jnp.maximum(margin, 0.0).reshape(SLAB // 8, 8, n_p), axis=0)
                gain = gain + (above - 0.5 * jnp.log(product))
            acc = acc + (gain + 0.5 * LOG2 * (n_s // 8)) * hazard[own, :]
        return acc

    def grad_block(i):
        blocks, rows = [], []
        for b in range(LAGMAX):
            t = i * LAGMAX + b
            for low in range(0, n_s, SLAB):
                at = pl.ds(low, SLAB)
                later = by_lag(lags16, [direct[t + lag, at] for lag in range(LAGMAX + 1)])
                blocks.append(direct[t, at] - later * gate[t, at])
            rows.append(fwd[t])
        total[...] += jnp.dot(
            jnp.concatenate(rows, axis=1),
            jnp.concatenate(blocks, axis=0),
            preferred_element_type=F32,
        )

    for b in range(LAGMAX):
        direct[b] = jnp.zeros((n_s, n_p), BF16)
        direct[steps + b] = jnp.zeros((n_s, n_p), BF16)
    total[...] = jnp.zeros((n_u, n_p), F32)

    last = steps // LAGMAX - 1
    value_block(0, after_first)
    value_block(1)
    acc = exposure_block(1, jnp.zeros((8, n_p), F32))
    value_block(2)

    def block_step(i, acc):
        grad_block(i - 3)
        acc = exposure_block(i - 1, acc)
        value_block(i)
        return acc

    acc = lax.fori_loop(3, last + 1, block_step, acc)
    acc = exposure_block(last, acc)
    terms = jnp.sum(acc, axis=0, keepdims=True) * (scales[0:1, :] * (2.0 / (RATE * paths)))
    charge_out[...] = exact_dot(jnp.broadcast_to(terms, (8, n_p)), named, NT)
    charges = []
    for k in range(1, n_group):
        charges.append(send(charge_out, charge_in.at[k], charge_sem, (k,), group_peer(k)))
    for i in range(last - 2, last + 1):
        grad_block(i)

    arrivals = []
    for k in range(1, n_group):
        theirs = pl.multiple_of(lax.rem(g + k, n_group) * uq, uq)
        arrivals.append(
            send(total.at[pl.ds(theirs, uq)], total_in.at[k], total_sem, (k,), group_peer(k))
        )

    for copy in charges:
        copy.wait_recv()
    pending += charges
    group_charge = charge_out[...]
    for k in range(1, n_group):
        group_charge = group_charge + charge_in[k]
    charge_sum[...] = group_charge
    charges = []
    for k in range(1, n_trade):
        charges.append(send(charge_sum, charge_far.at[k], far_sem, (k,), trade_peer(k)))

    for copy in arrivals:
        copy.wait_recv()
    pending += arrivals
    mine_sum = total[pl.ds(mine, uq), :]
    for k in range(1, n_group):
        mine_sum = mine_sum + total_in[k]
    every[z, pl.ds(mine, uq), :] = mine_sum.astype(BF16)

    block = every.at[z, pl.ds(mine, uq)]
    final = [send(block, block, every_sem, (j, k), peer(j, k)) for j, k in sorted(others, key=lambda p: (p[0], -p[1]))]
    for copy in charges:
        copy.wait_recv()
    pending += charges
    group_charge = charge_sum[...]
    for k in range(1, n_trade):
        group_charge = group_charge + charge_far[k]
    charge_ref[...] = group_charge[0:1, :]

    for copy in final:
        copy.wait_recv()
    pending += final
    rows = jnp.zeros((n_u, n_n), F32)
    for o in range(n_trade):
        rows = rows + jnp.dot(every[o], member[o * n_p : (o + 1) * n_p, :], preferred_element_type=F32)
    trade_rows[...] = rows

    def pick_step(i, out):
        base = pl.multiple_of(i * 8, 8)
        rows = trade_rows[pl.ds(base, 8), :]
        for b in range(8):
            out = jnp.where(moments == base + b, rows[b : b + 1, :], out)
        return out

    flows_ref[...] = lax.fori_loop(0, n_u // 8, pick_step, jnp.zeros((n_k, n_n), F32))
    for copy in pending:
        copy.wait_send()


def write_out(charge_ref, flows_ref, charge_out, flows_out, sems):
    copies = [
        pltpu.make_async_copy(flows_ref, flows_out, sems.at[0]),
        pltpu.make_async_copy(charge_ref, charge_out, sems.at[1]),
    ]
    for copy in copies:
        copy.start()
    for copy in copies:
        copy.wait()


def per_device(
    cash_flows,
    coupon_dates,
    trade_sets,
    set_slots,
    set_lags,
    thresholds,
    set_cpty,
    discounts,
    default_probs,
    loss_given,
    cva_cotangent,
):
    n_trade, n_date, n_scen = (lax.axis_size(a) for a in ("trade", "date", "scen"))
    n_group = n_date * n_scen
    n_n, n_k = cash_flows.shape
    span, n_u, n_s = discounts.shape
    n_p = set_lags.shape[0]
    n_sets = set_slots.shape[0]
    n_c = loss_given.shape[0]
    uq = n_u // n_group
    steps = span + LAGMAX
    vmem = pl.BlockSpec(memory_space=pltpu.VMEM)
    dma = pltpu.SemaphoreType.DMA
    charge, flow_grads = pl.pallas_call(
        functools.partial(kernel, n_trade, n_date, n_scen),
        out_shape=(
            jax.ShapeDtypeStruct((1, n_c), F32),
            jax.ShapeDtypeStruct((n_k, n_n), F32),
        ),
        in_specs=[pl.BlockSpec(memory_space=pltpu.HBM)] * 11,
        out_specs=(vmem, vmem),
        scratch_shapes=[
            pltpu.VMEM((n_k, n_n), cash_flows.dtype),
            pltpu.VMEM((n_k, n_n), jnp.int32),
            pltpu.VMEM((1, n_n), jnp.int32),
            pltpu.VMEM((1, n_sets), jnp.int32),
            pltpu.VMEM((1, n_p), jnp.int32),
            pltpu.VMEM((1, n_p), F32),
            pltpu.VMEM((1, n_p), jnp.int32),
            pltpu.VMEM((span, n_c), F32),
            pltpu.VMEM((1, n_c), F32),
            pltpu.VMEM((1, n_c), F32),
            pltpu.VMEM((steps, n_u, n_s), BF16),
            pltpu.VMEM((steps, n_s, n_u), BF16),
            pltpu.VMEM((steps, n_s, n_p), F32),
            pltpu.VMEM((steps, n_s, n_p), F32),
            pltpu.VMEM((steps, n_s, n_p), BF16),
            pltpu.VMEM((steps + LAGMAX, n_s, n_p), BF16),
            pltpu.VMEM((span, n_p), F32),
            pltpu.VMEM((span, n_p), F32),
            pltpu.VMEM((n_sets, n_n), BF16),
            pltpu.VMEM((n_trade, uq, n_p), F32),
            pltpu.VMEM((n_trade, uq, n_p), F32),
            pltpu.VMEM((n_u, n_p), BF16),
            pltpu.VMEM((n_u, n_p), F32),
            pltpu.VMEM((n_group, uq, n_p), F32),
            pltpu.VMEM((n_trade, n_u, n_p), BF16),
            pltpu.VMEM((n_u, n_n), F32),
            pltpu.VMEM((8, n_c), F32),
            pltpu.VMEM((n_group, 8, n_c), F32),
            pltpu.VMEM((8, n_c), F32),
            pltpu.VMEM((n_trade, 8, n_c), F32),
            dma,
            dma((10,)),
            dma((2,)),
            dma((2, n_trade)),
            dma((2, n_group)),
            dma((2, n_group)),
            dma((2, n_group)),
            dma((2, n_trade)),
            dma((2, n_trade, n_group)),
        ],
        compiler_params=pltpu.CompilerParams(
            collective_id=0, has_side_effects=True, vmem_limit_bytes=48 * 1024 * 1024
        ),
    )(
        *(
            pltpu.with_memory_space_constraint(a, pltpu.HBM)
            for a in (
                cash_flows.T,
                coupon_dates.T,
                trade_sets.reshape(1, -1),
                set_slots.reshape(1, -1),
                set_lags.reshape(1, -1),
                thresholds.reshape(1, -1),
                set_cpty.reshape(1, -1),
                default_probs.T,
                loss_given.reshape(1, -1),
                cva_cotangent.reshape(1, -1),
                discounts,
            )
        )
    )
    return charge.reshape(-1), flow_grads.T


def solution(mesh):
    in_specs = (
        P("trade", None),
        P("trade", None),
        P("trade"),
        P(),
        P("trade"),
        P("trade"),
        P("trade"),
        P("date", None, ("groups", "scen")),
        P(None, "date"),
        P(),
        P(),
    )
    out_specs = (P("groups"), P(("groups", "trade"), None))
    return jax.shard_map(
        per_device, mesh=mesh, in_specs=in_specs, out_specs=out_specs, check_vma=False
    )
```
